256 devices in a mesh: seg: 8 (over z), blk: 32 (over x, y, core).
Axes of the slice: x: 4, y: 4, z: 8, core: 2. Of those that a mesh axis runs over, the one named last changes fastest.
Arguments:
- train_acts: bfloat16 [8, 4096, 512], P('seg', 'blk'), may hold values from -6 to 6
- train_grads: bfloat16 [8, 4096, 16384], P('seg', 'blk'), may hold values from -0.0059814453 to 0.0059814453
- counts: int32 [32], replicated, may hold values from 1 to 2, as said below
- basis_in: bfloat16 [8, 1, 512, 512], P('seg'), may hold values from -1 to 1, as said below
- basis_out: bfloat16 [8, 32, 512, 512], P('seg', 'blk'), may hold values from -1 to 1, as said below
- eigenvalues: bfloat16 [8, 32, 512, 512], P('seg', 'blk'), may hold values from 0.049804688 to 5
- back_weight: bfloat16 [8, 32, 512, 512], P('seg', 'blk'), may hold values from -0.25 to 0.25
- derivative: bfloat16 [8, 4, 32, 16384], P('seg', None, None, 'blk'), may hold values from 0 to 1
- query_acts: bfloat16 [8, 4, 32, 512], P('seg'), may hold values from -6 to 6
- query_top: bfloat16 [4, 32, 16384], P(None, None, 'blk'), may hold values from -0.0059814453 to 0.0059814453
Outputs:
- scores: float32 [4, 64], P(None, 'blk')
The draws below stay inside these ranges and needn't reach their ends.
Inputs may be any that keep to these rules, and one draw needn't show every extreme that they name: In each pair of indices 2k and 2k+1 of blk one count is 2 and the other 1, so all counts add up to 48; slots below a device's count are valid. `basis_in`: each 512 x 512 matrix is orthogonal up to rounding. `basis_out`: each 512 x 512 matrix is orthogonal up to rounding.
All inputs are finite; a program needn't handle non-finite values.
Results may differ from the reference program's by a relative error of at most 0.015.
Values may be sent and summed in bfloat16 or wider, within the bound.
No kernel may reach another device: no remote copies, remote signals or barrier semaphores. Data moves between devices by JAX's collectives and lax.ppermute only.
A program may use at most 64 MiB of HBM per device.

```python
import math
import jax
import jax.numpy as jnp
from jax import lax

D_BLK = 512
IN_SL = 1
QUERIES = 4
QT = 32
TB = 64
SLOTS = 2
SEGS = 8
OUT_SL = 32
IN = 512
OUT = 16384
TOKENS = 4096


def draw_counts(key, part):
    which = jax.random.randint(jax.random.fold_in(key, 37), (OUT_SL // 2,), 0, 2).astype(jnp.int32)
    paired = jnp.stack([1 + which, 2 - which], axis=1)
    return paired.reshape(OUT_SL).astype(jnp.int32)


def draw_basis_in(key, part):
    raw = jax.random.normal(jax.random.fold_in(key, 11), (SEGS, IN_SL, D_BLK, D_BLK), jnp.float32)
    ortho, upper = jnp.linalg.qr(raw)
    return ortho.astype(jnp.bfloat16)


def draw_basis_out(key, part):
    raw = jax.random.normal(jax.random.fold_in(key, 23), (SEGS, OUT_SL, D_BLK, D_BLK), jnp.float32)
    ortho, upper = jnp.linalg.qr(raw)
    return ortho.astype(jnp.bfloat16)


def level_of(own_key, dims, pieces, least, largest):
    level = 1.0
    for position, blocks in pieces:
        heights = jax.random.uniform(jax.random.fold_in(jax.random.fold_in(own_key, 6), position), (blocks,), jnp.float32, least / len(pieces), largest / len(pieces))
        level = level * jnp.repeat(jnp.exp(heights), dims[position] // blocks).reshape((-1,) + (1,) * (len(dims) - 1 - position))
    return level


def normal_values(rng, shape, scale, bound, split=(), held_as=jnp.bfloat16):
    gain = level_of(rng, shape, split, -0.22, 0.18) if split else 1.0
    drawn = jax.random.normal(rng, shape, jnp.float32) * scale * gain
    return jnp.minimum(jnp.maximum(drawn, -bound), bound).astype(held_as)


def setup_inputs(seed: int = 0) -> dict:
    seeds = jax.random.split(jax.random.key(seed), 11)
    train_acts = normal_values(seeds[0], (SEGS, TOKENS, IN), 1.0, 6.0, ((0, 8), (1, 32)))
    train_grads = normal_values(seeds[1], (SEGS, TOKENS, OUT), 0.001, 0.0059814453, ((0, 8), (1, 32)))
    counts = draw_counts(jax.random.fold_in(seeds[10], 71), 0)
    basis_in = draw_basis_in(jax.random.fold_in(seeds[10], 71), 0)
    basis_out = draw_basis_out(jax.random.fold_in(seeds[10], 71), 0)
    eigenvalues = jnp.clip(jnp.exp(math.log(5.0) - 4.609084 * jax.random.uniform(seeds[5], (SEGS, OUT_SL, D_BLK, IN), jnp.float32) ** level_of(seeds[5], (SEGS, OUT_SL, D_BLK, IN), ((0, 8), (1, 32)), -0.2, 0.2)), 0.049804688, 5.0).astype(jnp.bfloat16)
    back_weight = normal_values(seeds[6], (SEGS, OUT_SL, D_BLK, D_BLK), D_BLK ** -0.5, 0.25, ((0, 8), (1, 32)))
    derivative = jnp.clip(1.0 * jax.random.uniform(seeds[7], (SEGS, QUERIES, QT, OUT), jnp.float32) ** level_of(seeds[7], (SEGS, QUERIES, QT, OUT), ((0, 8), (3, 32)), -0.2, 0.2), 0.0, 1.0).astype(jnp.bfloat16)
    query_acts = normal_values(seeds[8], (SEGS, QUERIES, QT, IN), 1.0, 6.0, ((0, 8),))
    query_top = normal_values(seeds[9], (QUERIES, QT, OUT), 0.001, 0.0059814453, ((2, 32),))
    return dict(train_acts=train_acts, train_grads=train_grads, counts=counts, basis_in=basis_in, basis_out=basis_out, eigenvalues=eigenvalues, back_weight=back_weight, derivative=derivative, query_acts=query_acts, query_top=query_top)


damping = 0.05

def reference(train_acts, train_grads, counts, basis_in, basis_out, eigenvalues, back_weight, derivative, query_acts, query_top):
    f32 = jnp.float32
    b16 = jnp.bfloat16
    seg_count = train_acts.shape[0]
    queries, query_tok, out_width = query_top.shape
    blk_width = basis_out.shape[-1]
    out_slices = basis_out.shape[1]
    in_slices = basis_in.shape[1]
    in_width = in_slices * blk_width
    n_slot = train_acts.shape[1] // TB
    current = query_top
    errors = [current]
    for segment in range(seg_count - 1, 0, -1):
        shaped = current.reshape(queries, query_tok, out_slices, blk_width).astype(f32)
        mixed = jnp.einsum('qtod,ode->qtoe', shaped, back_weight[segment].astype(f32))
        mixed = mixed.reshape(queries, query_tok, out_width)
        current = (current.astype(f32) + mixed * derivative[segment].astype(f32)).astype(b16)
        errors.insert(0, current)
    errors = jnp.stack(errors)

    def per_segment(operands):
        error_seg, acts_seg, inner_basis, outer_basis, eigen_seg, grads_train, acts_train = operands
        err_split = error_seg.reshape(queries, query_tok, out_slices, blk_width).astype(f32)
        rot_err = jnp.einsum('qtod,ode->qtoe', err_split, outer_basis.astype(f32)).astype(b16)
        act_split = acts_seg.reshape(queries, query_tok, in_slices, blk_width).astype(f32)
        rot_acts = jnp.einsum('qtid,ide->qtie', act_split, inner_basis.astype(f32)).astype(b16)
        core_raw = jnp.einsum('qtod,qtie->qodie', rot_err.astype(f32), rot_acts.astype(f32))
        core_raw = core_raw.reshape(queries, out_slices, blk_width, in_width)
        scaled_core = (core_raw / (eigen_seg.astype(f32)[None] + damping)).astype(b16)
        left_prod = jnp.einsum('ocd,qodf->qocf', outer_basis.astype(f32), scaled_core.astype(f32)).astype(b16)
        left_split = left_prod.reshape(queries, out_slices, blk_width, in_slices, blk_width)
        precond = jnp.einsum('qocie,ife->qocif', left_split.astype(f32), inner_basis.astype(f32))
        precond = precond.reshape(queries, out_slices, blk_width, in_width).astype(b16)
        act_slots = acts_train.reshape(n_slot, TB, in_width).astype(f32)
        grad_split = jnp.moveaxis(grads_train.reshape(n_slot * TB, out_slices, blk_width), 1, 0)
        precond_split = jnp.moveaxis(precond, 1, 0)

        def per_slice(slice_ops):
            grads_slice, precond_slice = slice_ops
            grad_slots = grads_slice.reshape(n_slot, TB, blk_width).astype(f32)
            outer_prod = jnp.einsum('ntd,nte->nde', grad_slots, act_slots).astype(b16)
            return jnp.einsum('nde,qde->qn', outer_prod.astype(f32), precond_slice.astype(f32))
        return jnp.sum(lax.map(per_slice, (grad_split, precond_split)), axis=0)
    seg_scores = lax.map(per_segment, (errors, query_acts, basis_in, basis_out, eigenvalues, train_grads, train_acts))
    summed = jnp.sum(seg_scores, axis=0)
    slot_ids = jnp.arange(n_slot, dtype=jnp.int32)
    valid = slot_ids % SLOTS < jnp.take(counts, slot_ids // SLOTS)
    return summed * valid.astype(f32)[None, :]
```

```python
import jax
import jax.numpy as jnp
from jax import lax
from jax.experimental import pallas as pl
from jax.experimental.pallas import tpu as pltpu
from jax.sharding import PartitionSpec as P

TB = 64
SLOTS = 2
HALF = TB // 2
ROWS = TB + HALF

damping = 0.05
f32 = jnp.float32
bf16 = jnp.bfloat16


def moved_one(value, axis, source, target):
    return lax.ppermute(value, axis, [(source, target)])


def swapped(value, axis):
    return lax.ppermute(value, axis, [(i, i ^ 1) for i in range(lax.axis_size(axis))])


def advance(current, weight, derivs):
    mixed = jnp.dot(current, weight, preferred_element_type=f32)
    return (current.astype(f32) + mixed * derivs.astype(f32)).astype(bf16)


def pack_kernel(count_ref, rows_ref, other_ref, derivs_ref, out_ref, passed_ref):
    width = out_ref.shape[2]
    both = count_ref[0] == SLOTS
    for i in range(out_ref.shape[0]):
        cols = pl.ds(i * width, width)
        out_ref[i, :TB, :] = rows_ref[:TB, cols]
        out_ref[i, TB:, :] = jnp.where(both, rows_ref[TB:ROWS, cols], other_ref[:, cols])
    passed_ref[...] = derivs_ref[...]


def pack(own_count, rows, other, derivs, width, step_slices):
    total = rows.shape[1]
    slices = total // width
    block = step_slices * width
    same = pl.BlockSpec(derivs.shape, lambda i, c: (0, 0))
    return pl.pallas_call(
        pack_kernel,
        grid_spec=pltpu.PrefetchScalarGridSpec(
            num_scalar_prefetch=1,
            grid=(slices // step_slices,),
            in_specs=[
                pl.BlockSpec((ROWS, block), lambda i, c: (0, i)),
                pl.BlockSpec((HALF, block), lambda i, c: (0, i)),
                same,
            ],
            out_specs=[
                pl.BlockSpec((step_slices, ROWS, width), lambda i, c: (i, 0, 0)),
                same,
            ],
        ),
        out_shape=[
            jax.ShapeDtypeStruct((slices, ROWS, width), bf16),
            jax.ShapeDtypeStruct(derivs.shape, bf16),
        ],
        compiler_params=pltpu.CompilerParams(vmem_limit_bytes=32 * 1024 * 1024),
        cost_estimate=pl.CostEstimate(
            flops=0, bytes_accessed=4 * slices * ROWS * width, transcendentals=0
        ),
    )(own_count, rows, other, derivs)


def acts_kernel(count_ref, rows_ref, other_ref, basis_ref, out_ref):
    both = count_ref[0] == SLOTS
    basis = basis_ref[...]
    out_ref[:TB, :] = jnp.dot(rows_ref[:TB, :], basis, preferred_element_type=f32).astype(bf16)
    rest = jnp.where(both, rows_ref[TB:ROWS, :], other_ref[...])
    out_ref[TB:, :] = jnp.dot(rest, basis, preferred_element_type=f32).astype(bf16)


def rotated_acts(own_count, rows, other, basis):
    width = rows.shape[1]
    vmem = pl.BlockSpec(memory_space=pltpu.VMEM)
    return pl.pallas_call(
        acts_kernel,
        in_specs=[pl.BlockSpec(memory_space=pltpu.SMEM), vmem, vmem, vmem],
        out_specs=vmem,
        out_shape=jax.ShapeDtypeStruct((ROWS, width), bf16),
        cost_estimate=pl.CostEstimate(
            flops=2 * ROWS * width * width, bytes_accessed=2 * width * (width + 3 * ROWS), transcendentals=0
        ),
    )(own_count, rows, other, basis)


def core_kernel(err_ref, qacts_ref, bin_ref, bout_ref, eig_ref, core_ref):
    queries = core_ref.shape[0]
    query_tok = err_ref.shape[0] // queries
    rot_err = jnp.dot(err_ref[...], bout_ref[...], preferred_element_type=f32).astype(bf16)
    rot_acts = jnp.dot(qacts_ref[...], bin_ref[...], preferred_element_type=f32).astype(bf16)
    inverse = 1.0 / (eig_ref[...].astype(f32) + damping)
    for q in range(queries):
        tokens = slice(q * query_tok, (q + 1) * query_tok)
        raw = lax.dot_general(
            rot_err[tokens], rot_acts[tokens], (((0,), (0,)), ((), ())),
            preferred_element_type=f32,
        )
        core_ref[q] = (raw * inverse).astype(bf16)


def scaled_core(err, qacts, basis_in, basis_out, eigen, queries):
    width = basis_out.shape[0]
    vmem = pl.BlockSpec(memory_space=pltpu.VMEM)
    return pl.pallas_call(
        core_kernel,
        in_specs=[vmem] * 5,
        out_specs=vmem,
        out_shape=jax.ShapeDtypeStruct((queries, width, width), bf16),
        compiler_params=pltpu.CompilerParams(vmem_limit_bytes=24 * 1024 * 1024),
        cost_estimate=pl.CostEstimate(
            flops=6 * err.shape[0] * width * width,
            bytes_accessed=(6 + 2 * queries) * width * width,
            transcendentals=0,
        ),
    )(err, qacts, basis_in, basis_out, eigen)


def score_kernel(core_ref, bout_ref, place_ref, grads_ref, acts_ref, out_ref, acc_ref):
    step = pl.program_id(0)
    queries = out_ref.shape[0]
    width = bout_ref.shape[0]
    groups = grads_ref.shape[0] // HALF

    grads = jnp.dot(grads_ref[...], bout_ref[...], preferred_element_type=f32).astype(bf16)
    acts = acts_ref[...].astype(f32)
    at = pl.multiple_of(step * groups, groups)
    for q in range(queries):
        mapped = jnp.dot(grads, core_ref[q], preferred_element_type=f32)
        summed = (mapped * acts).reshape(groups, HALF, width).sum(axis=1)
        acc_ref[q, pl.ds(at, groups), :] = summed

    @pl.when(step == pl.num_programs(0) - 1)
    def _():
        for q in range(queries):
            by_slot = jnp.dot(
                place_ref[...], acc_ref[q], precision=lax.Precision.HIGHEST,
                preferred_element_type=f32,
            )
            out_ref[q] = jnp.broadcast_to(
                by_slot.sum(axis=1, keepdims=True), out_ref.shape[1:]
            )


def block_scores(core, basis_out, placement, grads, acts, tile):
    rows, width = grads.shape
    queries = core.shape[0]
    slots = placement.shape[0]
    lanes = 128
    whole = lambda a: pl.BlockSpec(a.shape, lambda i: (0,) * a.ndim)
    streamed = pl.BlockSpec((tile, width), lambda i: (i, 0))
    return pl.pallas_call(
        score_kernel,
        grid=(rows // tile,),
        in_specs=[whole(core), whole(basis_out), whole(placement), streamed, streamed],
        out_specs=pl.BlockSpec((queries, slots, lanes), lambda i: (0, 0, 0)),
        out_shape=jax.ShapeDtypeStruct((queries, slots, lanes), f32),
        scratch_shapes=[pltpu.VMEM((queries, rows // HALF, width), f32)],
        compiler_params=pltpu.CompilerParams(vmem_limit_bytes=48 * 1024 * 1024),
        cost_estimate=pl.CostEstimate(
            flops=2 * rows * width * width * (queries + 1),
            bytes_accessed=4 * rows * width,
            transcendentals=0,
        ),
    )(core, basis_out, placement, grads, acts)


def body(
    train_acts, train_grads, counts, basis_in, basis_out, eigenvalues, back_weight,
    derivative, query_acts, query_top,
):
    seg_count = lax.axis_size("seg")
    seg_index = lax.axis_index("seg")
    blk_count = lax.axis_size("blk")
    blk_index = lax.axis_index("blk")
    queries, query_tok, width = query_top.shape
    own_count = lax.dynamic_slice_in_dim(counts, blk_index, 1)

    pieces = ROWS // HALF
    holder = jnp.arange(blk_count * pieces, dtype=jnp.int32) // pieces
    piece = jnp.arange(blk_count * pieces, dtype=jnp.int32) % pieces
    pair_first = jnp.repeat(counts.reshape(-1, 2)[:, 0] == SLOTS, 2 * pieces)
    extra = (holder // 2) * 2 * SLOTS + jnp.where(pair_first, 1, SLOTS + 1)
    slot_of = jnp.where(piece < TB // HALF, holder * SLOTS, extra)
    slot_ids = jnp.arange(blk_count * SLOTS, dtype=jnp.int32)
    placement = (slot_ids[:, None] == slot_of[None, :]).astype(f32)

    acts_other = swapped(train_acts[0, ROWS:], "blk")
    grads_other = swapped(train_grads[0, ROWS:], "blk")
    acts_own = rotated_acts(own_count, train_acts[0], acts_other, basis_in[0, 0])
    acts_rows = lax.all_gather(acts_own, "blk", axis=0, tiled=True)

    derivs = derivative[0].reshape(queries * query_tok, width)
    packed, late_derivs = pack(own_count, train_grads[0], grads_other, derivs, width, 4)
    grad_rows = lax.all_to_all(packed, "blk", split_axis=0, concat_axis=0, tiled=True)
    grad_rows = grad_rows.reshape(blk_count * ROWS, width)

    current = query_top.reshape(queries * query_tok, width)
    kept = current
    for relay_step in range(seg_count - 1):
        segment = seg_count - 1 - relay_step
        moved = advance(current, back_weight[0, 0], late_derivs if relay_step else derivs)
        current = moved_one(moved, "seg", segment, segment - 1)
        kept = jnp.where(seg_index == segment - 1, current, kept)

    core = scaled_core(
        kept, query_acts[0].reshape(queries * query_tok, width),
        basis_in[0, 0], basis_out[0, 0], eigenvalues[0, 0], queries,
    )
    part = block_scores(core, basis_out[0, 0], placement, grad_rows, acts_rows, 8 * ROWS)
    part = part[:, :, 0].T.reshape(blk_count, SLOTS * queries)
    mine = lax.all_to_all(part, "blk", split_axis=0, concat_axis=0, tiled=True).sum(axis=0)
    copies = jnp.broadcast_to(mine[None], (seg_count, SLOTS * queries))
    mine = lax.all_to_all(copies, "seg", split_axis=0, concat_axis=0, tiled=True).sum(axis=0)
    return mine.reshape(SLOTS, queries).T


def solution(mesh):
    in_specs = (
        P("seg", "blk", None),
        P("seg", "blk", None),
        P(),
        P("seg", None, None, None),
        P("seg", "blk", None, None),
        P("seg", "blk", None, None),
        P("seg", "blk", None, None),
        P("seg", None, None, "blk"),
        P("seg", None, None, None),
        P(None, None, "blk"),
    )
    out_specs = P(None, "blk")
    return jax.shard_map(body, mesh=mesh, in_specs=in_specs, out_specs=out_specs, check_vma=False)
```

```python
import jax
import jax.numpy as jnp
from jax import lax
from jax.experimental import pallas as pl
from jax.experimental.pallas import tpu as pltpu
from jax.sharding import PartitionSpec as P

TB = 64
SLOTS = 2
HALF = TB // 2
ROWS = TB + HALF

damping = 0.05
f32 = jnp.float32
bf16 = jnp.bfloat16


def moved_one(value, axis, source, target):
    return lax.ppermute(value, axis, [(source, target)])


def swapped(value, axis):
    return lax.ppermute(value, axis, [(i, i ^ 1) for i in range(lax.axis_size(axis))])


def advance(current, weight, derivs):
    mixed = jnp.dot(current, weight, preferred_element_type=f32)
    return (current.astype(f32) + mixed * derivs.astype(f32)).astype(bf16)


def pack_kernel(count_ref, rows_ref, other_ref, derivs_ref, out_ref, passed_ref):
    width = out_ref.shape[2]
    both = count_ref[lax.axis_index("blk")] == SLOTS
    for i in range(out_ref.shape[0]):
        cols = pl.ds(i * width, width)
        out_ref[i, :TB, :] = rows_ref[:TB, cols]
        out_ref[i, TB:, :] = jnp.where(both, rows_ref[TB:ROWS, cols], other_ref[:, cols])
    passed_ref[...] = derivs_ref[...]


def pack(all_counts, rows, other, derivs, width, step_slices):
    total = rows.shape[1]
    slices = total // width
    block = step_slices * width
    same = pl.BlockSpec(derivs.shape, lambda i, c: (0, 0))
    return pl.pallas_call(
        pack_kernel,
        grid_spec=pltpu.PrefetchScalarGridSpec(
            num_scalar_prefetch=1,
            grid=(slices // step_slices,),
            in_specs=[
                pl.BlockSpec((ROWS, block), lambda i, c: (0, i)),
                pl.BlockSpec((HALF, block), lambda i, c: (0, i)),
                same,
            ],
            out_specs=[
                pl.BlockSpec((step_slices, ROWS, width), lambda i, c: (i, 0, 0)),
                same,
            ],
        ),
        out_shape=[
            jax.ShapeDtypeStruct((slices, ROWS, width), bf16),
            jax.ShapeDtypeStruct(derivs.shape, bf16),
        ],
        compiler_params=pltpu.CompilerParams(vmem_limit_bytes=32 * 1024 * 1024),
        cost_estimate=pl.CostEstimate(
            flops=0, bytes_accessed=4 * slices * ROWS * width, transcendentals=0
        ),
    )(all_counts, rows, other, derivs)


def acts_kernel(count_ref, rows_ref, other_ref, basis_ref, out_ref):
    both = count_ref[lax.axis_index("blk")] == SLOTS
    basis = basis_ref[...]
    out_ref[:TB, :] = jnp.dot(rows_ref[:TB, :], basis, preferred_element_type=f32).astype(bf16)
    rest = jnp.where(both, rows_ref[TB:ROWS, :], other_ref[...])
    out_ref[TB:, :] = jnp.dot(rest, basis, preferred_element_type=f32).astype(bf16)


def rotated_acts(all_counts, rows, other, basis):
    width = rows.shape[1]
    vmem = pl.BlockSpec(memory_space=pltpu.VMEM)
    return pl.pallas_call(
        acts_kernel,
        in_specs=[pl.BlockSpec(memory_space=pltpu.SMEM), vmem, vmem, vmem],
        out_specs=vmem,
        out_shape=jax.ShapeDtypeStruct((ROWS, width), bf16),
        cost_estimate=pl.CostEstimate(
            flops=2 * ROWS * width * width, bytes_accessed=2 * width * (width + 3 * ROWS), transcendentals=0
        ),
    )(all_counts, rows, other, basis)


def core_kernel(err_ref, qacts_ref, bin_ref, bout_ref, eig_ref, core_ref):
    queries = core_ref.shape[0]
    query_tok = err_ref.shape[0] // queries
    rot_err = jnp.dot(err_ref[...], bout_ref[...], preferred_element_type=f32).astype(bf16)
    rot_acts = jnp.dot(qacts_ref[...], bin_ref[...], preferred_element_type=f32).astype(bf16)
    inverse = 1.0 / (eig_ref[...].astype(f32) + damping)
    for q in range(queries):
        tokens = slice(q * query_tok, (q + 1) * query_tok)
        raw = lax.dot_general(
            rot_err[tokens], rot_acts[tokens], (((0,), (0,)), ((), ())),
            preferred_element_type=f32,
        )
        core_ref[q] = (raw * inverse).astype(bf16)


def scaled_core(err, qacts, basis_in, basis_out, eigen, queries):
    width = basis_out.shape[0]
    vmem = pl.BlockSpec(memory_space=pltpu.VMEM)
    return pl.pallas_call(
        core_kernel,
        in_specs=[vmem] * 5,
        out_specs=vmem,
        out_shape=jax.ShapeDtypeStruct((queries, width, width), bf16),
        compiler_params=pltpu.CompilerParams(vmem_limit_bytes=24 * 1024 * 1024),
        cost_estimate=pl.CostEstimate(
            flops=6 * err.shape[0] * width * width,
            bytes_accessed=(6 + 2 * queries) * width * width,
            transcendentals=0,
        ),
    )(err, qacts, basis_in, basis_out, eigen)


def score_kernel(core_ref, bout_ref, place_ref, grads_ref, acts_ref, out_ref, acc_ref):
    step = pl.program_id(0)
    queries = out_ref.shape[0]
    width = bout_ref.shape[0]
    groups = grads_ref.shape[0] // HALF

    grads = jnp.dot(grads_ref[...], bout_ref[...], preferred_element_type=f32).astype(bf16)
    acts = acts_ref[...].astype(f32)
    at = pl.multiple_of(step * groups, groups)
    for q in range(queries):
        mapped = jnp.dot(grads, core_ref[q], preferred_element_type=f32)
        summed = (mapped * acts).reshape(groups, HALF, width).sum(axis=1)
        acc_ref[q, pl.ds(at, groups), :] = summed

    @pl.when(step == pl.num_programs(0) - 1)
    def _():
        for q in range(queries):
            by_slot = jnp.dot(
                place_ref[...], acc_ref[q], precision=lax.Precision.HIGHEST,
                preferred_element_type=f32,
            )
            out_ref[q] = jnp.broadcast_to(
                by_slot.sum(axis=1, keepdims=True), out_ref.shape[1:]
            )


def block_scores(core, basis_out, placement, grads, acts, tile):
    rows, width = grads.shape
    queries = core.shape[0]
    slots = placement.shape[0]
    lanes = 128
    whole = lambda a: pl.BlockSpec(a.shape, lambda i: (0,) * a.ndim)
    streamed = pl.BlockSpec((tile, width), lambda i: (i, 0))
    return pl.pallas_call(
        score_kernel,
        grid=(rows // tile,),
        in_specs=[whole(core), whole(basis_out), whole(placement), streamed, streamed],
        out_specs=pl.BlockSpec((queries, slots, lanes), lambda i: (0, 0, 0)),
        out_shape=jax.ShapeDtypeStruct((queries, slots, lanes), f32),
        scratch_shapes=[pltpu.VMEM((queries, rows // HALF, width), f32)],
        compiler_params=pltpu.CompilerParams(vmem_limit_bytes=48 * 1024 * 1024),
        cost_estimate=pl.CostEstimate(
            flops=2 * rows * width * width * (queries + 1),
            bytes_accessed=4 * rows * width,
            transcendentals=0,
        ),
    )(core, basis_out, placement, grads, acts)


def body(
    train_acts, train_grads, counts, basis_in, basis_out, eigenvalues, back_weight,
    derivative, query_acts, query_top,
):
    seg_count = lax.axis_size("seg")
    seg_index = lax.axis_index("seg")
    blk_count = lax.axis_size("blk")
    blk_index = lax.axis_index("blk")
    queries, query_tok, width = query_top.shape
    all_counts = counts

    pieces = ROWS // HALF
    holder = jnp.arange(blk_count * pieces, dtype=jnp.int32) // pieces
    piece = jnp.arange(blk_count * pieces, dtype=jnp.int32) % pieces
    pair_first = jnp.repeat(counts.reshape(-1, 2)[:, 0] == SLOTS, 2 * pieces)
    extra = (holder // 2) * 2 * SLOTS + jnp.where(pair_first, 1, SLOTS + 1)
    slot_of = jnp.where(piece < TB // HALF, holder * SLOTS, extra)
    slot_ids = jnp.arange(blk_count * SLOTS, dtype=jnp.int32)
    placement = (slot_ids[:, None] == slot_of[None, :]).astype(f32)

    acts_other = swapped(train_acts[0, ROWS:], "blk")
    grads_other = swapped(train_grads[0, ROWS:], "blk")
    acts_own = rotated_acts(all_counts, train_acts[0], acts_other, basis_in[0, 0])
    acts_rows = lax.all_gather(acts_own, "blk", axis=0, tiled=True)

    derivs = derivative[0].reshape(queries * query_tok, width)
    packed, late_derivs = pack(all_counts, train_grads[0], grads_other, derivs, width, 4)
    grad_rows = lax.all_to_all(packed, "blk", split_axis=0, concat_axis=0, tiled=True)
    grad_rows = grad_rows.reshape(blk_count * ROWS, width)

    current = query_top.reshape(queries * query_tok, width)
    kept = current
    for relay_step in range(seg_count - 1):
        segment = seg_count - 1 - relay_step
        moved = advance(current, back_weight[0, 0], late_derivs if relay_step else derivs)
        current = moved_one(moved, "seg", segment, segment - 1)
        kept = jnp.where(seg_index == segment - 1, current, kept)

    core = scaled_core(
        kept, query_acts[0].reshape(queries * query_tok, width),
        basis_in[0, 0], basis_out[0, 0], eigenvalues[0, 0], queries,
    )
    part = block_scores(core, basis_out[0, 0], placement, grad_rows, acts_rows, 8 * ROWS)
    part = part[:, :, 0].T.reshape(blk_count, SLOTS * queries)
    mine = lax.all_to_all(part, "blk", split_axis=0, concat_axis=0, tiled=True).sum(axis=0)
    copies = jnp.broadcast_to(mine[None], (seg_count, SLOTS * queries))
    mine = lax.all_to_all(copies, "seg", split_axis=0, concat_axis=0, tiled=True).sum(axis=0)
    return mine.reshape(SLOTS, queries).T


def solution(mesh):
    in_specs = (
        P("seg", "blk", None),
        P("seg", "blk", None),
        P(),
        P("seg", None, None, None),
        P("seg", "blk", None, None),
        P("seg", "blk", None, None),
        P("seg", "blk", None, None),
        P("seg", None, None, "blk"),
        P("seg", None, None, None),
        P(None, None, "blk"),
    )
    out_specs = P(None, "blk")
    return jax.shard_map(body, mesh=mesh, in_specs=in_specs, out_specs=out_specs, check_vma=False)
```
